512 devices in a mesh: reg: 16 (over z, core), prod: 32 (over x, y).
Axes of the slice: x: 4, y: 8, z: 8, core: 2. Of those that a mesh axis runs over, the one named last changes fastest.
Arguments:
- panel_factor: float32 [131072, 2048], P('reg', 'prod'), may hold values from -0.125 to 0.125
- block_inverse: float32 [2048, 2048], P('prod', 'reg'), may hold values from -1 to 2.5
- panel_rhs: float32 [2048, 1024], P('reg'), may hold values from -6 to 6
- trailing_rhs: float32 [131072, 1024], P(('reg', 'prod')), may hold values from -6 to 6
Outputs:
- solved: float32 [2048, 1024], P('prod', 'reg')
- updated: float32 [131072, 1024], P(('reg', 'prod'))
The draws below stay inside these ranges and needn't reach their ends.
All inputs are finite; a program needn't handle non-finite values.
Results may differ from the reference program's by a relative error of at most 0.000075.
Values sent between devices are 32-bit elements; how exact they have to be, the bound alone decides.
A program may use at most 64 MiB of HBM per device.

```python
import jax
import jax.numpy as jnp
from jax import lax

PANEL = 2048
RHS = 1024
TRAIL = 131072


def draw_block_inverse(key, part):
    key = jax.random.fold_in(key, 7)
    first, second = jax.random.split(key)
    spread = 0.6 / jnp.sqrt(jnp.float32(PANEL))
    off = jax.random.truncated_normal(first, -4.0, 4.0, (PANEL, PANEL), jnp.float32) * spread
    logs = jax.random.uniform(second, (PANEL,), jnp.float32, jnp.log(0.5), jnp.log(2.0))
    rows = lax.broadcasted_iota(jnp.int32, (PANEL, PANEL), 0)
    cols = lax.broadcasted_iota(jnp.int32, (PANEL, PANEL), 1)
    diag = jnp.where(rows == cols, jnp.exp(logs)[:, None], 0.0)
    return (off + diag).astype(jnp.float32)


def steps_of(key, extent, pieces, least, high):
    def one(position, shards_of):
        steps = jax.random.uniform(jax.random.fold_in(jax.random.fold_in(key, 6), position), (shards_of,), jnp.float32, least / len(pieces), high / len(pieces))
        return jnp.repeat(jnp.exp(steps), extent[position] // shards_of).reshape((-1,) + (1,) * (len(extent) - position - 1))

    factor_of = one(*pieces[0])
    for cut in pieces[1:]:
        factor_of = factor_of * one(*cut)
    return factor_of


def scatter_about(own_key, extent, scale, most, pieces=(), held_as=jnp.bfloat16):
    drawn = jax.random.normal(own_key, extent, jnp.float32) * scale
    if len(pieces) > 0:
        drawn = steps_of(own_key, extent, pieces, -0.22, 0.18) * drawn
    return jnp.clip(drawn, min=-most, max=most).astype(held_as)


def setup_inputs(seed: int = 0) -> dict:
    seeds = jax.random.split(jax.random.key(seed), 5)
    panel_factor = scatter_about(seeds[0], (TRAIL, PANEL), PANEL ** -0.5, 0.125, ((0, 16), (1, 32)), jnp.float32)
    block_inverse = draw_block_inverse(jax.random.fold_in(seeds[4], 71), 0)
    panel_rhs = scatter_about(seeds[2], (PANEL, RHS), 1.0, 6.0, ((0, 16),), jnp.float32)
    trailing_rhs = scatter_about(seeds[3], (TRAIL, RHS), 1.0, 6.0, ((0, 512),), jnp.float32)
    return dict(panel_factor=panel_factor, block_inverse=block_inverse, panel_rhs=panel_rhs, trailing_rhs=trailing_rhs)


def reference(panel_factor, block_inverse, panel_rhs, trailing_rhs):
    solved = jnp.dot(block_inverse, panel_rhs, precision=lax.Precision.HIGHEST, preferred_element_type=jnp.float32)
    updated = trailing_rhs - jnp.dot(panel_factor, solved, precision=lax.Precision.HIGHEST, preferred_element_type=jnp.float32)
    return solved, updated
```

```python
import functools

import jax
import jax.numpy as jnp
from jax import lax
from jax.experimental import pallas as pl
from jax.experimental.pallas import tpu as pltpu
from jax.sharding import PartitionSpec as P

MESH = pl.DeviceIdType.MESH
NX, NY, NZ = 4, 8, 8
F32, BF16 = jnp.float32, jnp.bfloat16


def kernel(
    ft_ref, b_ref, p_ref, t_ref, solved_ref, out_ref,
    b_v, p_v, t_v, o_v, sv_v, part, landed, g, fg, a_hi, a_lo, s_hi, s_lo,
    loc_sem, o_sem, rs_s, rs_r, f_s, f_r, y_s, y_r, x_s, x_r, z_s, z_r, c_s, c_r,
):
    reg, prod = lax.axis_index("reg"), lax.axis_index("prod")
    z, c = reg // 2, reg % 2
    x, y = prod // NY, prod % NY
    sibling = z * 2 + 1 - c

    def send(src, dst, s, r, to_reg, to_prod):
        return pltpu.make_async_remote_copy(
            src_ref=src, dst_ref=dst, send_sem=s, recv_sem=r,
            device_id=(to_reg, to_prod), device_id_type=MESH,
        )

    load_b = pltpu.make_async_copy(b_ref, b_v, loc_sem.at[0])
    load_p = pltpu.make_async_copy(p_ref, p_v, loc_sem.at[1])
    load_t = pltpu.make_async_copy(t_ref, t_v, loc_sem.at[2])
    load_f = pltpu.make_async_copy(
        ft_ref.at[:, :, pl.ds(pl.multiple_of(prod * 256, 256), 256)], fg.at[:, prod], loc_sem.at[3]
    )
    load_b.start()
    load_p.start()

    barrier = pltpu.get_barrier_semaphore()
    for d in range(1, 2 * NZ):
        pl.semaphore_signal(barrier, inc=1, device_id=((reg + d) % (2 * NZ), prod), device_id_type=MESH)
    for d in range(1, NX * NY):
        pl.semaphore_signal(barrier, inc=1, device_id=(reg, (prod + d) % (NX * NY)), device_id_type=MESH)

    load_b.wait()
    load_p.wait()
    product = jnp.dot(b_v[...], p_v[...], precision=lax.Precision.HIGHEST, preferred_element_type=F32)
    for i in range(2 * NZ):
        part[i] = product[(i % 2) * 32:(i % 2) * 32 + 32, (i // 2) * 128:(i // 2) * 128 + 128]

    pl.semaphore_wait(barrier, 2 * NZ - 1 + NX * NY - 1)

    sends = []

    def go(copy):
        copy.start()
        sends.append(copy)

    rs = []
    for d in range(1, 2 * NZ):
        to = (reg + d) % (2 * NZ)
        copy = send(part.at[to], landed.at[reg], rs_s.at[d], rs_r.at[d], to, prod)
        go(copy)
        rs.append(copy)

    factor = []
    for dy in (4, 3, 5, 2, 6, 1, 7, 0):
        for dx in (2, 1, 3, 0):
            if dx == 0 and dy == 0:
                continue
            to = ((x + dx) % NX) * NY + (y + dy) % NY
            i = dx * NY + dy
            copy = send(
                ft_ref.at[:, :, pl.ds(pl.multiple_of(to * 256, 256), 256)],
                fg.at[:, prod], f_s.at[i], f_r.at[i], reg, to,
            )
            go(copy)
            factor.append(copy)
    load_f.start()
    load_t.start()

    landed[reg] = part[reg]
    for copy in rs:
        copy.wait_recv()
    g[z, c, prod] = jnp.sum(landed[...], axis=0)

    ys = []
    for dy in (1, 7, 2, 6, 3, 5, 4):
        copy = send(
            g.at[z, c, prod], g.at[z, c, prod], y_s.at[dy], y_r.at[dy], reg, x * NY + (y + dy) % NY
        )
        go(copy)
        ys.append(copy)
    for copy in ys:
        copy.wait_recv()

    def unit(zs, cs, j):
        return g.at[zs, cs, pl.ds(((x + j) % NX) * NY, NY)]

    def relay(zs, slot, j, right, left):
        u = unit(zs, c, j)
        if right is not None:
            go(send(u, u, z_s.at[0, right, j], z_r.at[0, right, j], ((z + 1) % NZ) * 2 + c, prod))
        if left is not None:
            go(send(u, u, z_s.at[1, left, j], z_r.at[1, left, j], ((z + NZ - 1) % NZ) * 2 + c, prod))
        go(send(u, u, c_s.at[slot, j], c_r.at[slot, j], sibling, prod))

    xs = {}
    for dx in (1, 3, 2):
        u = unit(z, c, 0)
        copy = send(u, u, x_s.at[dx], x_r.at[dx], reg, ((x + dx) % NX) * NY + y)
        go(copy)
        xs[(NX - dx) % NX] = copy
    relay(z, 0, 0, 0, 0)
    for j in (1, 3, 2):
        xs[j].wait_recv()
        relay(z, 0, j, 0, 0)

    def arrive(way, hop, j):
        zs = (z + NZ - hop) % NZ if way == 0 else (z + hop) % NZ
        u = unit(zs, c, j)
        send(u, u, z_s.at[way, hop - 1, j], z_r.at[way, hop - 1, j], reg, prod).wait_recv()
        onward = hop < 3 or (hop == 3 and (j < 2) == (way == 0))
        slot = 7 if hop == 4 else hop + 3 * way
        relay(
            zs, slot, j,
            hop if way == 0 and onward else None,
            hop if way == 1 and onward else None,
        )

    def from_sibling(slot, zs):
        for j in range(NX):
            u = unit(zs, 1 - c, j)
            send(u, u, c_s.at[slot, j], c_r.at[slot, j], reg, prod).wait_recv()

    def factor_in():
        load_f.wait()
        for copy in factor:
            copy.wait_recv()
        for cs in range(2):
            for j in range(NX):
                block = fg[cs, j * NY:(j + 1) * NY].reshape(256, 256).T
                hi = block.astype(BF16)
                k = (cs * NX + j) * 256
                a_hi[:, k:k + 256] = hi
                a_lo[:, k:k + 256] = (block - hi.astype(F32)).astype(BF16)

    def multiply(za, zb):
        for half, zs in enumerate((za, zb)):
            block = g[zs].reshape(2048, 128)
            hi = block.astype(BF16)
            s_hi[:, half * 128:half * 128 + 128] = hi
            s_lo[:, half * 128:half * 128 + 128] = (block - hi.astype(F32)).astype(BF16)
        acc = jnp.dot(a_hi[...], s_lo[...], preferred_element_type=F32)
        acc += jnp.dot(a_lo[...], s_hi[...], preferred_element_type=F32)
        acc += jnp.dot(a_hi[...], s_hi[...], preferred_element_type=F32)
        for half, zs in enumerate((za, zb)):
            cols = pl.ds(pl.multiple_of(zs * 128, 128), 128)
            o_v[:, cols] = t_v[:, cols] - acc[:, half * 128:half * 128 + 128]

    for hop in (1, 2, 3):
        for j in (0, 1, 3, 2):
            arrive(0, hop, j)
            arrive(1, hop, j)
    for j in range(NX):
        arrive(0 if j < 2 else 1, 4, j)

    from_sibling(0, z)
    own = jnp.concatenate([g[z, 0, prod], g[z, 1, prod]], axis=0)
    sv_v[...] = jnp.where(c == 0, own[:, :64], own[:, 64:])
    store_s = pltpu.make_async_copy(sv_v, solved_ref, loc_sem.at[4])
    store_s.start()

    load_t.wait()
    factor_in()
    for hop in (1, 2, 3):
        za, zb = (z + NZ - hop) % NZ, (z + hop) % NZ
        from_sibling(hop, za)
        from_sibling(hop + 3, zb)
        multiply(za, zb)
    from_sibling(7, (z + 4) % NZ)
    multiply(z, (z + 4) % NZ)
    store = pltpu.make_async_copy(o_v, out_ref, o_sem.at[0])
    store.start()
    for copy in sends:
        copy.wait_send()
    store.wait()
    store_s.wait()


def local(panel_factor, block_inverse, panel_rhs, trailing_rhs):
    ft = panel_factor.T.reshape(2, 32, 8192)
    dma = pltpu.SemaphoreType.DMA
    any_spec = pl.BlockSpec(memory_space=pl.ANY)
    return pl.pallas_call(
        kernel,
        out_shape=(
            jax.ShapeDtypeStruct((64, 64), F32),
            jax.ShapeDtypeStruct((256, 1024), F32),
        ),
        in_specs=[any_spec] * 4,
        out_specs=(any_spec, any_spec),
        scratch_shapes=[
            pltpu.VMEM((64, 128), F32),
            pltpu.VMEM((128, 1024), F32),
            pltpu.VMEM((256, 1024), F32),
            pltpu.VMEM((256, 1024), F32),
            pltpu.VMEM((64, 64), F32),
            pltpu.VMEM((16, 32, 128), F32),
            pltpu.VMEM((16, 32, 128), F32),
            pltpu.VMEM((8, 2, 32, 32, 128), F32),
            pltpu.VMEM((2, 32, 32, 256), F32),
            pltpu.VMEM((256, 2048), BF16),
            pltpu.VMEM((256, 2048), BF16),
            pltpu.VMEM((2048, 256), BF16),
            pltpu.VMEM((2048, 256), BF16),
            dma((5,)),
            dma((1,)),
            dma((16,)),
            dma((16,)),
            dma((32,)),
            dma((32,)),
            dma((8,)),
            dma((8,)),
            dma((4,)),
            dma((4,)),
            dma((2, 4, 4)),
            dma((2, 4, 4)),
            dma((8, 4)),
            dma((8, 4)),
        ],
        compiler_params=pltpu.CompilerParams(
            collective_id=0, has_side_effects=True, vmem_limit_bytes=40 * 1024 * 1024
        ),
        name="panel_step",
    )(ft, block_inverse, panel_rhs, trailing_rhs)


def solution(mesh):
    in_specs = (P("reg", "prod"), P("prod", "reg"), P("reg", None), P(("reg", "prod"), None))
    out_specs = (P("prod", "reg"), P(("reg", "prod"), None))
    return jax.shard_map(local, mesh=mesh, in_specs=in_specs, out_specs=out_specs, check_vma=False)
```

```python
import functools

import jax
import jax.numpy as jnp
from jax import lax
from jax.experimental import pallas as pl
from jax.experimental.pallas import tpu as pltpu
from jax.sharding import PartitionSpec as P

MESH = pl.DeviceIdType.MESH
NX, NY, NZ = 4, 8, 8
F32, BF16 = jnp.float32, jnp.bfloat16


def split(block):
    hi = block.astype(BF16)
    return hi, (block - hi.astype(F32)).astype(BF16)


def dot3(a_hi, a_lo, b_hi, b_lo):
    acc = jnp.dot(a_hi, b_lo, preferred_element_type=F32)
    acc += jnp.dot(a_lo, b_hi, preferred_element_type=F32)
    return acc + jnp.dot(a_hi, b_hi, preferred_element_type=F32)


FIRST, SECOND, EACH = 4, 0, 1


def kernel(
    ft_ref, b_ref, p_ref, t_ref, solved_ref, out_ref,
    b_v, p_v, acc, sv_v, part, landed, g, fg, a_hi, a_lo, s_hi, s_lo,
    loc_sem, t_sem, o_sem, rs_s, rs_r, f_s, f_r, y_s, y_r, x_s, x_r, z_s, z_r, c_s, c_r,
):
    reg, prod = lax.axis_index("reg"), lax.axis_index("prod")
    z, c = reg // 2, reg % 2
    x, y = prod // NY, prod % NY
    sibling = z * 2 + 1 - c

    def send(src, dst, s, r, to_reg, to_prod):
        return pltpu.make_async_remote_copy(
            src_ref=src, dst_ref=dst, send_sem=s, recv_sem=r,
            device_id=(to_reg, to_prod), device_id_type=MESH,
        )

    load_b = pltpu.make_async_copy(b_ref, b_v, loc_sem.at[0])
    load_p = pltpu.make_async_copy(p_ref, p_v, loc_sem.at[1])
    load_f = pltpu.make_async_copy(
        ft_ref.at[:, :, pl.ds(pl.multiple_of(prod * 256, 256), 256)], fg.at[:, prod], loc_sem.at[2]
    )
    load_b.start()
    load_p.start()

    barrier = pltpu.get_barrier_semaphore()
    for d in range(1, 2 * NZ):
        pl.semaphore_signal(barrier, inc=1, device_id=((reg + d) % (2 * NZ), prod), device_id_type=MESH)
    for d in range(1, NX * NY):
        pl.semaphore_signal(barrier, inc=1, device_id=(reg, (prod + d) % (NX * NY)), device_id_type=MESH)

    def chunk_of(slot):
        if slot < 4:
            return (z + NZ - slot) % NZ
        return (z + slot - 3) % NZ

    def columns(slot):
        return pl.ds(pl.multiple_of(chunk_of(slot) * 128, 128), 128)

    load_b.wait()
    load_p.wait()
    product = dot3(*split(b_v[...]), *split(p_v[...]))
    for i in range(2 * NZ):
        part[i] = product[(i % 2) * 32:(i % 2) * 32 + 32, (i // 2) * 128:(i // 2) * 128 + 128]

    pl.semaphore_wait(barrier, 2 * NZ - 1 + NX * NY - 1)

    sends = []

    def go(copy):
        copy.start()
        sends.append(copy)

    rs = []
    for d in range(1, 2 * NZ):
        to = (reg + d) % (2 * NZ)
        copy = send(part.at[to], landed.at[reg], rs_s.at[d], rs_r.at[d], to, prod)
        go(copy)
        rs.append(copy)

    factor, queue = {}, []
    for dx in (0, 1, 3, 2):
        for dy in (4, 3, 5, 2, 6, 1, 7, 0):
            if dx == 0 and dy == 0:
                continue
            to = ((x + dx) % NX) * NY + (y + dy) % NY
            i = dx * NY + dy
            copy = send(
                ft_ref.at[:, :, pl.ds(pl.multiple_of(to * 256, 256), 256)],
                fg.at[:, prod], f_s.at[i], f_r.at[i], reg, to,
            )
            queue.append(copy)
            factor.setdefault((NX - dx) % NX, []).append(copy)

    def pump(count):
        for _ in range(min(count, len(queue))):
            go(queue.pop(0))

    pump(FIRST)
    load_f.start()
    loads = []
    for slot in range(NZ):
        loads.append(pltpu.make_async_copy(t_ref.at[:, columns(slot)], acc.at[slot], t_sem.at[slot]))
        loads[-1].start()

    landed[reg] = part[reg]
    for copy in rs:
        copy.wait_recv()
    g[z, c, prod] = jnp.sum(landed[...], axis=0)

    ys = []
    for dy in (1, 7, 2, 6, 3, 5, 4):
        copy = send(
            g.at[z, c, prod], g.at[z, c, prod], y_s.at[dy], y_r.at[dy], reg, x * NY + (y + dy) % NY
        )
        go(copy)
        ys.append(copy)
    pump(SECOND)
    for copy in ys:
        copy.wait_recv()

    def unit(zs, cs, j):
        return g.at[zs, cs, pl.ds(((x + j) % NX) * NY, NY)]

    def relay(slot, j, right, left):
        u = unit(chunk_of(slot), c, j)
        if right is not None:
            go(send(u, u, z_s.at[0, right, j], z_r.at[0, right, j], ((z + 1) % NZ) * 2 + c, prod))
        if left is not None:
            go(send(u, u, z_s.at[1, left, j], z_r.at[1, left, j], ((z + NZ - 1) % NZ) * 2 + c, prod))
        go(send(u, u, c_s.at[slot, j], c_r.at[slot, j], sibling, prod))
        pump(EACH)

    xs = {}
    for dx in (1, 3, 2):
        u = unit(z, c, 0)
        copy = send(u, u, x_s.at[dx], x_r.at[dx], reg, ((x + dx) % NX) * NY + y)
        go(copy)
        xs[(NX - dx) % NX] = copy
    relay(0, 0, 0, 0)
    for j in (1, 3, 2):
        xs[j].wait_recv()
        relay(0, j, 0, 0)

    def arrive(way, hop, j):
        slot = 7 if hop == 4 else hop + 3 * way
        u = unit(chunk_of(slot), c, j)
        send(u, u, z_s.at[way, hop - 1, j], z_r.at[way, hop - 1, j], reg, prod).wait_recv()
        onward = hop < 3 or (hop == 3 and (j < 2) == (way == 0))
        relay(
            slot, j,
            hop if way == 0 and onward else None,
            hop if way == 1 and onward else None,
        )

    pairs = ((1, 4), (2, 5), (3, 6), (0, 7))

    def chunk_in(pair, half):
        slot = pairs[pair][half]
        for j in range(NX):
            u = unit(chunk_of(slot), 1 - c, j)
            send(u, u, c_s.at[slot, j], c_r.at[slot, j], reg, prod).wait_recv()
            for cs in range(2):
                hi, lo = split(unit(chunk_of(slot), cs, j)[...].reshape(256, 128))
                s_hi[pair, j, cs * 256:cs * 256 + 256, half * 128:half * 128 + 128] = hi
                s_lo[pair, j, cs * 256:cs * 256 + 256, half * 128:half * 128 + 128] = lo

    def factor_in(j):
        if j == 0:
            load_f.wait()
        for copy in factor[j]:
            copy.wait_recv()
        for cs in range(2):
            block = fg[cs, pl.ds(((x + j) % NX) * NY, NY)].reshape(256, 256).T
            hi, lo = split(block)
            a_hi[j, :, cs * 256:cs * 256 + 256] = hi
            a_lo[j, :, cs * 256:cs * 256 + 256] = lo

    def multiply(j, pair):
        term = dot3(a_hi[j], a_lo[j], s_hi[pair, j], s_lo[pair, j])
        for half, slot in enumerate(pairs[pair]):
            acc[slot] -= term[:, half * 128:half * 128 + 128]

    def hops(hop):
        for j in (0, 1, 3, 2):
            arrive(0, hop, j)
            arrive(1, hop, j)

    hops(1)
    chunk_in(3, 0)
    own = jnp.concatenate([g[z, 0, prod], g[z, 1, prod]], axis=0)
    sv_v[...] = jnp.where(c == 0, own[:, :64], own[:, 64:])
    store_s = pltpu.make_async_copy(sv_v, solved_ref, loc_sem.at[3])
    store_s.start()
    for copy in loads:
        copy.wait()
    factor_in(0)
    hops(2)
    chunk_in(0, 0)
    chunk_in(0, 1)
    multiply(0, 0)
    factor_in(3)
    multiply(3, 0)
    hops(3)
    pump(31)
    for j in range(NX):
        arrive(0 if j < 2 else 1, 4, j)
    chunk_in(1, 0)
    chunk_in(1, 1)
    multiply(0, 1)
    multiply(3, 1)
    factor_in(1)
    multiply(1, 0)
    multiply(1, 1)
    chunk_in(2, 0)
    chunk_in(2, 1)
    for j in (0, 3, 1):
        multiply(j, 2)
    chunk_in(3, 1)
    for j in (0, 3, 1):
        multiply(j, 3)
    factor_in(2)
    stores = []
    for pair in range(4):
        multiply(2, pair)
        for slot in pairs[pair]:
            stores.append(pltpu.make_async_copy(acc.at[slot], out_ref.at[:, columns(slot)], o_sem.at[slot]))
            stores[-1].start()
    for copy in sends:
        copy.wait_send()
    for copy in stores:
        copy.wait()
    store_s.wait()


def local(panel_factor, block_inverse, panel_rhs, trailing_rhs):
    ft = panel_factor.T.reshape(2, 32, 8192)
    dma = pltpu.SemaphoreType.DMA
    any_spec = pl.BlockSpec(memory_space=pl.ANY)
    return pl.pallas_call(
        kernel,
        out_shape=(
            jax.ShapeDtypeStruct((64, 64), F32),
            jax.ShapeDtypeStruct((256, 1024), F32),
        ),
        in_specs=[any_spec] * 4,
        out_specs=(any_spec, any_spec),
        scratch_shapes=[
            pltpu.VMEM((64, 128), F32),
            pltpu.VMEM((128, 1024), F32),
            pltpu.VMEM((8, 256, 128), F32),
            pltpu.VMEM((64, 64), F32),
            pltpu.VMEM((16, 32, 128), F32),
            pltpu.VMEM((16, 32, 128), F32),
            pltpu.VMEM((8, 2, 32, 32, 128), F32),
            pltpu.VMEM((2, 32, 32, 256), F32),
            pltpu.VMEM((4, 256, 512), BF16),
            pltpu.VMEM((4, 256, 512), BF16),
            pltpu.VMEM((4, 4, 512, 256), BF16),
            pltpu.VMEM((4, 4, 512, 256), BF16),
            dma((4,)),
            dma((8,)),
            dma((8,)),
            dma((16,)),
            dma((16,)),
            dma((32,)),
            dma((32,)),
            dma((8,)),
            dma((8,)),
            dma((4,)),
            dma((4,)),
            dma((2, 4, 4)),
            dma((2, 4, 4)),
            dma((8, 4)),
            dma((8, 4)),
        ],
        compiler_params=pltpu.CompilerParams(
            collective_id=0, has_side_effects=True, vmem_limit_bytes=60 * 1024 * 1024
        ),
        name="panel_step",
    )(ft, block_inverse, panel_rhs, trailing_rhs)


def solution(mesh):
    in_specs = (P("reg", "prod"), P("prod", "reg"), P("reg", None), P(("reg", "prod"), None))
    out_specs = (P("prod", "reg"), P(("reg", "prod"), None))
    return jax.shard_map(local, mesh=mesh, in_specs=in_specs, out_specs=out_specs, check_vma=False)
```

```python
import functools

import jax
import jax.numpy as jnp
from jax import lax
from jax.experimental import pallas as pl
from jax.experimental.pallas import tpu as pltpu
from jax.sharding import PartitionSpec as P

MESH = pl.DeviceIdType.MESH
NX, NY, NZ = 4, 8, 8
F32, BF16 = jnp.float32, jnp.bfloat16


def split(block):
    hi = block.astype(BF16)
    return hi, (block - hi.astype(F32)).astype(BF16)


def dot3(a_hi, a_lo, b_hi, b_lo):
    acc = jnp.dot(a_hi, b_lo, preferred_element_type=F32)
    acc += jnp.dot(a_lo, b_hi, preferred_element_type=F32)
    return acc + jnp.dot(a_hi, b_hi, preferred_element_type=F32)


FIRST, SECOND, EACH = 4, 0, 1


def kernel(
    ft_ref, b_ref, p_ref, t_ref, solved_ref, out_ref,
    b_v, p_v, acc, sv_v, part, landed, g, fg, a_hi, a_lo, s_hi, s_lo,
    loc_sem, t_sem, o_sem, rs_s, rs_r, f_s, f_r, y_s, y_r, x_s, x_r, z_s, z_r, c_s, c_r,
):
    reg, prod = lax.axis_index("reg"), lax.axis_index("prod")
    z, c = reg // 2, reg % 2
    x, y = prod // NY, prod % NY
    sibling = z * 2 + 1 - c

    def send(src, dst, s, r, to_reg, to_prod):
        return pltpu.make_async_remote_copy(
            src_ref=src, dst_ref=dst, send_sem=s, recv_sem=r,
            device_id=(to_reg, to_prod), device_id_type=MESH,
        )

    load_b = pltpu.make_async_copy(b_ref, b_v, loc_sem.at[0])
    load_p = pltpu.make_async_copy(p_ref, p_v, loc_sem.at[1])
    load_f = pltpu.make_async_copy(
        ft_ref.at[:, :, pl.ds(pl.multiple_of(prod * 256, 256), 256)], fg.at[:, prod], loc_sem.at[2]
    )
    load_b.start()
    load_p.start()

    barrier = pltpu.get_barrier_semaphore()
    for d in range(1, 2 * NZ):
        pl.semaphore_signal(barrier, inc=1, device_id=((reg + d) % (2 * NZ), prod), device_id_type=MESH)
    for d in range(1, NX * NY):
        pl.semaphore_signal(barrier, inc=1, device_id=(reg, (prod + d) % (NX * NY)), device_id_type=MESH)

    def chunk_of(slot):
        if slot < 4:
            return (z + NZ - slot) % NZ
        return (z + slot - 3) % NZ

    def columns(slot):
        return pl.ds(pl.multiple_of(chunk_of(slot) * 128, 128), 128)

    load_b.wait()
    load_p.wait()
    product = dot3(*split(b_v[...]), *split(p_v[...]))
    for i in range(2 * NZ):
        part[i] = product[(i % 2) * 32:(i % 2) * 32 + 32, (i // 2) * 128:(i // 2) * 128 + 128]

    pl.semaphore_wait(barrier, 2 * NZ - 1 + NX * NY - 1)

    sends = []

    def go(copy):
        copy.start()
        sends.append(copy)

    rs = []
    for d in range(1, 2 * NZ):
        to = (reg + d) % (2 * NZ)
        copy = send(part.at[to], landed.at[reg], rs_s.at[d], rs_r.at[d], to, prod)
        go(copy)
        rs.append(copy)

    factor, queue = {}, []
    for dx in (0, 1, 3, 2):
        for dy in (4, 3, 5, 2, 6, 1, 7, 0):
            if dx == 0 and dy == 0:
                continue
            to = ((x + dx) % NX) * NY + (y + dy) % NY
            i = dx * NY + dy
            copy = send(
                ft_ref.at[:, :, pl.ds(pl.multiple_of(to * 256, 256), 256)],
                fg.at[:, prod], f_s.at[i], f_r.at[i], reg, to,
            )
            queue.append(copy)
            factor.setdefault((NX - dx) % NX, []).append(copy)

    def pump(count):
        for _ in range(min(count, len(queue))):
            go(queue.pop(0))

    pump(FIRST)
    load_f.start()
    loads = []
    for slot in range(NZ):
        loads.append(pltpu.make_async_copy(t_ref.at[:, columns(slot)], acc.at[slot], t_sem.at[slot]))
        loads[-1].start()

    landed[reg] = part[reg]
    for copy in rs:
        copy.wait_recv()
    g[z, c, prod] = jnp.sum(landed[...], axis=0)

    ys = []
    for dy in (1, 7, 2, 6, 3, 5, 4):
        copy = send(
            g.at[z, c, prod], g.at[z, c, prod], y_s.at[dy], y_r.at[dy], reg, x * NY + (y + dy) % NY
        )
        go(copy)
        ys.append(copy)
    pump(SECOND)
    for copy in ys:
        copy.wait_recv()

    def unit(zs, cs, j):
        return g.at[zs, cs, pl.ds(((x + j) % NX) * NY, NY)]

    def relay(slot, j, right, left):
        u = unit(chunk_of(slot), c, j)
        if right is not None:
            go(send(u, u, z_s.at[0, right, j], z_r.at[0, right, j], ((z + 1) % NZ) * 2 + c, prod))
        if left is not None:
            go(send(u, u, z_s.at[1, left, j], z_r.at[1, left, j], ((z + NZ - 1) % NZ) * 2 + c, prod))
        go(send(u, u, c_s.at[slot, j], c_r.at[slot, j], sibling, prod))
        pump(EACH)

    xs = {}
    for dx in (1, 3, 2):
        u = unit(z, c, 0)
        copy = send(u, u, x_s.at[dx], x_r.at[dx], reg, ((x + dx) % NX) * NY + y)
        go(copy)
        xs[(NX - dx) % NX] = copy
    relay(0, 0, 0, 0)
    for j in (1, 3, 2):
        xs[j].wait_recv()
        relay(0, j, 0, 0)

    def arrive(way, hop, j):
        slot = 7 if hop == 4 else hop + 3 * way
        u = unit(chunk_of(slot), c, j)
        send(u, u, z_s.at[way, hop - 1, j], z_r.at[way, hop - 1, j], reg, prod).wait_recv()
        onward = hop < 3 or (hop == 3 and (j < 2) == (way == 0))
        relay(
            slot, j,
            hop if way == 0 and onward else None,
            hop if way == 1 and onward else None,
        )

    pairs = ((1, 4), (2, 5), (3, 6), (0, 7))

    def chunk_in(pair, half):
        slot = pairs[pair][half]
        for j in range(NX):
            u = unit(chunk_of(slot), 1 - c, j)
            send(u, u, c_s.at[slot, j], c_r.at[slot, j], reg, prod).wait_recv()
            for cs in range(2):
                hi, lo = split(unit(chunk_of(slot), cs, j)[...].reshape(256, 128))
                s_hi[pair, j, cs * 256:cs * 256 + 256, half * 128:half * 128 + 128] = hi
                s_lo[pair, j, cs * 256:cs * 256 + 256, half * 128:half * 128 + 128] = lo

    def factor_in(j):
        if j == 0:
            load_f.wait()
        for copy in factor[j]:
            copy.wait_recv()
        for cs in range(2):
            block = fg[cs, pl.ds(((x + j) % NX) * NY, NY)].reshape(256, 256).T
            hi, lo = split(block)
            a_hi[j, :, cs * 256:cs * 256 + 256] = hi
            a_lo[j, :, cs * 256:cs * 256 + 256] = lo

    def multiply(j, pair):
        term = dot3(a_hi[j], a_lo[j], s_hi[pair, j], s_lo[pair, j])
        for half, slot in enumerate(pairs[pair]):
            acc[slot] -= term[:, half * 128:half * 128 + 128]

    def hops(hop):
        for j in (0, 1, 3, 2):
            arrive(0, hop, j)
            arrive(1, hop, j)

    hops(1)
    chunk_in(3, 0)
    own = jnp.concatenate([g[z, 0, prod], g[z, 1, prod]], axis=0)
    sv_v[...] = jnp.where(c == 0, own[:, :64], own[:, 64:])
    store_s = pltpu.make_async_copy(sv_v, solved_ref, loc_sem.at[3])
    store_s.start()
    for copy in loads:
        copy.wait()
    factor_in(0)
    hops(2)
    chunk_in(0, 0)
    chunk_in(0, 1)
    multiply(0, 0)
    factor_in(3)
    multiply(3, 0)
    hops(3)
    pump(31)
    chunk_in(1, 0)
    chunk_in(1, 1)
    multiply(0, 1)
    multiply(3, 1)
    arrive(0, 4, 0)
    arrive(1, 4, 3)
    chunk_in(2, 0)
    chunk_in(2, 1)
    multiply(0, 2)
    multiply(3, 2)
    arrive(0, 4, 1)
    arrive(1, 4, 2)
    factor_in(1)
    for pair in range(3):
        multiply(1, pair)
    chunk_in(3, 1)
    for j in (0, 3, 1):
        multiply(j, 3)
    factor_in(2)
    stores = []
    for pair in range(4):
        multiply(2, pair)
        for slot in pairs[pair]:
            stores.append(pltpu.make_async_copy(acc.at[slot], out_ref.at[:, columns(slot)], o_sem.at[slot]))
            stores[-1].start()
    for copy in sends:
        copy.wait_send()
    for copy in stores:
        copy.wait()
    store_s.wait()


def local(panel_factor, block_inverse, panel_rhs, trailing_rhs):
    ft = panel_factor.T.reshape(2, 32, 8192)
    dma = pltpu.SemaphoreType.DMA
    any_spec = pl.BlockSpec(memory_space=pl.ANY)
    return pl.pallas_call(
        kernel,
        out_shape=(
            jax.ShapeDtypeStruct((64, 64), F32),
            jax.ShapeDtypeStruct((256, 1024), F32),
        ),
        in_specs=[any_spec] * 4,
        out_specs=(any_spec, any_spec),
        scratch_shapes=[
            pltpu.VMEM((64, 128), F32),
            pltpu.VMEM((128, 1024), F32),
            pltpu.VMEM((8, 256, 128), F32),
            pltpu.VMEM((64, 64), F32),
            pltpu.VMEM((16, 32, 128), F32),
            pltpu.VMEM((16, 32, 128), F32),
            pltpu.VMEM((8, 2, 32, 32, 128), F32),
            pltpu.VMEM((2, 32, 32, 256), F32),
            pltpu.VMEM((4, 256, 512), BF16),
            pltpu.VMEM((4, 256, 512), BF16),
            pltpu.VMEM((4, 4, 512, 256), BF16),
            pltpu.VMEM((4, 4, 512, 256), BF16),
            dma((4,)),
            dma((8,)),
            dma((8,)),
            dma((16,)),
            dma((16,)),
            dma((32,)),
            dma((32,)),
            dma((8,)),
            dma((8,)),
            dma((4,)),
            dma((4,)),
            dma((2, 4, 4)),
            dma((2, 4, 4)),
            dma((8, 4)),
            dma((8, 4)),
        ],
        compiler_params=pltpu.CompilerParams(
            collective_id=0, has_side_effects=True, vmem_limit_bytes=60 * 1024 * 1024
        ),
        name="panel_step",
    )(ft, block_inverse, panel_rhs, trailing_rhs)


def solution(mesh):
    in_specs = (P("reg", "prod"), P("prod", "reg"), P("reg", None), P(("reg", "prod"), None))
    out_specs = (P("prod", "reg"), P(("reg", "prod"), None))
    return jax.shard_map(local, mesh=mesh, in_specs=in_specs, out_specs=out_specs, check_vma=False)
```

```python
import functools

import jax
import jax.numpy as jnp
from jax import lax
from jax.experimental import pallas as pl
from jax.experimental.pallas import tpu as pltpu
from jax.sharding import PartitionSpec as P

MESH = pl.DeviceIdType.MESH
NX, NY, NZ = 4, 8, 8
F32, BF16 = jnp.float32, jnp.bfloat16


def split(block):
    hi = block.astype(BF16)
    return hi, (block - hi.astype(F32)).astype(BF16)


def dot3(a_hi, a_lo, b_hi, b_lo):
    acc = jnp.dot(a_hi, b_lo, preferred_element_type=F32)
    acc += jnp.dot(a_lo, b_hi, preferred_element_type=F32)
    return acc + jnp.dot(a_hi, b_hi, preferred_element_type=F32)


FIRST, SECOND, EACH = 4, 3, 1


def kernel(
    ft_ref, b_ref, p_ref, t_ref, solved_ref, out_ref,
    b_v, p_v, acc, sv_v, part, paired, landed, g, fx, fg, a_hi, a_lo, s_hi, s_lo,
    loc_sem, t_sem, o_sem, rs_s, rs_r, fx_s, fx_r, f_s, f_r, y_s, y_r, x_s, x_r, z_s, z_r, w_s, w_r, c_s, c_r,
):
    reg, prod = lax.axis_index("reg"), lax.axis_index("prod")
    z, c = reg // 2, reg % 2
    x, y = prod // NY, prod % NY
    sibling = z * 2 + 1 - c

    def send(src, dst, s, r, to_reg, to_prod):
        return pltpu.make_async_remote_copy(
            src_ref=src, dst_ref=dst, send_sem=s, recv_sem=r,
            device_id=(to_reg, to_prod), device_id_type=MESH,
        )

    load_b = pltpu.make_async_copy(b_ref, b_v, loc_sem.at[0])
    load_p = pltpu.make_async_copy(p_ref, p_v, loc_sem.at[1])
    load_f = pltpu.make_async_copy(
        ft_ref.at[:, :, pl.ds(pl.multiple_of(prod * 256, 256), 256)], fg.at[:, prod], loc_sem.at[2]
    )
    load_b.start()
    load_p.start()

    barrier = pltpu.get_barrier_semaphore()
    pl.semaphore_signal(barrier, inc=1, device_id=(sibling, prod), device_id_type=MESH)
    for d in range(1, NZ):
        pl.semaphore_signal(barrier, inc=1, device_id=((reg + 2 * d) % (2 * NZ), prod), device_id_type=MESH)
    for d in range(1, NX):
        pl.semaphore_signal(barrier, inc=1, device_id=(reg, ((x + d) % NX) * NY + y), device_id_type=MESH)
    for d in range(1, NY):
        pl.semaphore_signal(barrier, inc=1, device_id=(reg, x * NY + (y + d) % NY), device_id_type=MESH)

    def chunk_of(slot):
        if slot < 4:
            return (z + NZ - slot) % NZ
        return (z + slot - 3) % NZ

    def columns(slot):
        return pl.ds(pl.multiple_of(chunk_of(slot) * 128, 128), 128)

    load_b.wait()
    load_p.wait()
    product = dot3(*split(b_v[...]), *split(p_v[...]))
    for i in range(2 * NZ):
        part[i % 2, i // 2] = product[(i % 2) * 32:(i % 2) * 32 + 32, (i // 2) * 128:(i // 2) * 128 + 128]

    pl.semaphore_wait(barrier, NZ + NX - 1 + NY - 1)

    sends = []

    def go(copy):
        copy.start()
        sends.append(copy)

    pair = send(part.at[1 - c], paired, rs_s.at[0], rs_r.at[0], sibling, prod)
    go(pair)

    stage = {}
    for dx in (1, 3, 2):
        j = NX - dx
        to = (x + dx) % NX
        stage[j] = send(
            ft_ref.at[:, :, pl.ds(pl.multiple_of(to * 2048, 2048), 2048)],
            fx.at[j], fx_s.at[j], fx_r.at[j], reg, to * NY + y,
        )
    factor, queue = {}, []
    for j in (0, 3, 1, 2):
        for dy in (4, 3, 5, 2, 6, 1, 7):
            to = (y + dy) % NY
            if j == 0:
                src = ft_ref.at[:, :, pl.ds(pl.multiple_of((x * NY + to) * 256, 256), 256)]
            else:
                src = fx.at[j, :, :, pl.ds(pl.multiple_of(to * 256, 256), 256)]
            copy = send(
                src, fg.at[:, ((x + j) % NX) * NY + y], f_s.at[j, dy], f_r.at[j, dy], reg, x * NY + to
            )
            queue.append((j, copy))
            factor.setdefault(j, []).append(copy)
    landing = set()

    def pump(count):
        for _ in range(min(count, len(queue))):
            j, copy = queue.pop(0)
            if j > 0 and j not in landing:
                landing.add(j)
                stage[j].wait_recv()
                own_rows = fx.at[j, :, :, pl.ds(pl.multiple_of(y * 256, 256), 256)]
                keep = pltpu.make_async_copy(own_rows, fg.at[:, ((x + j) % NX) * NY + y], f_r.at[j, 0])
                keep.start()
                kept[j] = keep
            go(copy)

    kept = {}

    pair.wait_recv()
    part[c] += paired[...]
    rs = []
    for d in (4, 3, 5, 2, 6, 1, 7):
        to = (z + d) % NZ
        copy = send(part.at[c, to], landed.at[z], rs_s.at[d], rs_r.at[d], to * 2 + c, prod)
        go(copy)
        rs.append(copy)

    pump(FIRST)
    go(stage[3])
    go(stage[1])
    load_f.start()
    loads = []
    for slot in range(NZ):
        loads.append(pltpu.make_async_copy(t_ref.at[:, columns(slot)], acc.at[slot], t_sem.at[slot]))
        loads[-1].start()

    landed[z] = part[c, z]
    for copy in rs:
        copy.wait_recv()
    g[z, c, prod] = jnp.sum(landed[...], axis=0)

    ys = []
    for dy in (1, 7, 2, 6, 3, 5, 4):
        copy = send(
            g.at[z, c, prod], g.at[z, c, prod], y_s.at[dy], y_r.at[dy], reg, x * NY + (y + dy) % NY
        )
        go(copy)
        ys.append(copy)
    pump(SECOND)
    for copy in ys:
        copy.wait_recv()

    def unit(zs, cs, j):
        return g.at[zs, cs, pl.ds(((x + j) % NX) * NY, NY)]

    def relay(slot, j, right, left):
        u = unit(chunk_of(slot), c, j)
        if right is not None:
            go(send(u, u, z_s.at[0, right, j], z_r.at[0, right, j], ((z + 1) % NZ) * 2 + c, prod))
        if left is not None:
            go(send(u, u, z_s.at[1, left, j], z_r.at[1, left, j], ((z + NZ - 1) % NZ) * 2 + c, prod))
        go(send(u, u, c_s.at[slot, j], c_r.at[slot, j], sibling, prod))
        pump(EACH)

    def along_x(slot, steps):
        u = unit(chunk_of(slot), c, 0)
        for dx in steps:
            j = (NX - dx) % NX
            go(send(u, u, x_s.at[slot, j], x_r.at[slot, j], reg, ((x + dx) % NX) * NY + y))

    def from_x(slot, j):
        u = unit(chunk_of(slot), c, j)
        send(u, u, x_s.at[slot, j], x_r.at[slot, j], reg, prod).wait_recv()

    def arrive(way, hop, j):
        slot = hop + 3 * way
        u = unit(chunk_of(slot), c, j)
        send(u, u, z_s.at[way, hop - 1, j], z_r.at[way, hop - 1, j], reg, prod).wait_recv()
        onward = hop == 1 or (hop == 2 and j in (0, 2))
        relay(
            slot, j,
            hop if way == 0 and onward else None,
            hop if way == 1 and onward else None,
        )

    along_x(0, (1, 3, 2))
    relay(0, 0, 0, 0)
    from_x(0, 1)
    relay(0, 1, 0, 0)
    arrive(0, 1, 0)
    arrive(1, 1, 0)
    from_x(0, 3)
    relay(0, 3, 0, 0)
    arrive(0, 2, 0)
    arrive(1, 2, 0)
    from_x(0, 2)
    relay(0, 2, 0, 0)
    go(stage[2])
    for way in range(2):
        arrive(way, 3, 0)
        along_x(3 + 3 * way, (1, 3))
    u = unit((z + NZ - 3 + 6 * c) % NZ, c, 0)
    go(send(u, u, w_s.at[0], w_r.at[0], ((z + NZ + 1 - 2 * c) % NZ) * 2 + c, prod))
    u = unit(chunk_of(7), c, 0)
    send(u, u, w_s.at[0], w_r.at[0], reg, prod).wait_recv()
    along_x(7, (1, 3, 2))
    relay(7, 0, None, None)
    for j in (1, 3, 2):
        arrive(0, 1, j)
        arrive(1, 1, j)

    pairs = ((1, 4), (2, 5), (3, 6), (0, 7))

    def chunk_in(pair, half):
        slot = pairs[pair][half]
        for j in range(NX):
            u = unit(chunk_of(slot), 1 - c, j)
            send(u, u, c_s.at[slot, j], c_r.at[slot, j], reg, prod).wait_recv()
            for cs in range(2):
                hi, lo = split(unit(chunk_of(slot), cs, j)[...].reshape(256, 128))
                s_hi[pair, j, cs * 256:cs * 256 + 256, half * 128:half * 128 + 128] = hi
                s_lo[pair, j, cs * 256:cs * 256 + 256, half * 128:half * 128 + 128] = lo

    def factor_in(j):
        if j == 0:
            load_f.wait()
        else:
            kept[j].wait()
        for copy in factor[j]:
            copy.wait_recv()
        for cs in range(2):
            block = fg[cs, pl.ds(((x + j) % NX) * NY, NY)].reshape(256, 256).T
            hi, lo = split(block)
            a_hi[j, :, cs * 256:cs * 256 + 256] = hi
            a_lo[j, :, cs * 256:cs * 256 + 256] = lo

    def multiply(j, pair):
        term = dot3(a_hi[j], a_lo[j], s_hi[pair, j], s_lo[pair, j])
        for half, slot in enumerate(pairs[pair]):
            acc[slot] -= term[:, half * 128:half * 128 + 128]

    chunk_in(3, 0)
    own = jnp.concatenate([g[z, 0, prod], g[z, 1, prod]], axis=0)
    sv_v[...] = jnp.where(c == 0, own[:, :64], own[:, 64:])
    store_s = pltpu.make_async_copy(sv_v, solved_ref, loc_sem.at[3])
    store_s.start()
    for copy in loads:
        copy.wait()
    factor_in(0)
    for j in (1, 3, 2):
        arrive(0, 2, j)
        arrive(1, 2, j)
    pump(31)
    chunk_in(0, 0)
    chunk_in(0, 1)
    multiply(0, 0)
    chunk_in(1, 0)
    chunk_in(1, 1)
    multiply(0, 1)
    factor_in(3)
    multiply(3, 0)
    multiply(3, 1)
    for slot, j in ((3, 1), (6, 1), (3, 3), (6, 3), (7, 1), (7, 3), (7, 2)):
        from_x(slot, j)
        relay(slot, j, None, None)
    arrive(0, 3, 2)
    arrive(1, 3, 2)
    factor_in(1)
    multiply(1, 0)
    multiply(1, 1)
    chunk_in(2, 0)
    chunk_in(2, 1)
    for j in (0, 3, 1):
        multiply(j, 2)
    chunk_in(3, 1)
    for j in (0, 3, 1):
        multiply(j, 3)
    factor_in(2)
    stores = []
    for pair in range(4):
        multiply(2, pair)
        for slot in pairs[pair]:
            stores.append(pltpu.make_async_copy(acc.at[slot], out_ref.at[:, columns(slot)], o_sem.at[slot]))
            stores[-1].start()
    for copy in sends:
        copy.wait_send()
    for copy in stores:
        copy.wait()
    store_s.wait()


def local(panel_factor, block_inverse, panel_rhs, trailing_rhs):
    ft = panel_factor.T.reshape(2, 32, 8192)
    dma = pltpu.SemaphoreType.DMA
    any_spec = pl.BlockSpec(memory_space=pl.ANY)
    return pl.pallas_call(
        kernel,
        out_shape=(
            jax.ShapeDtypeStruct((64, 64), F32),
            jax.ShapeDtypeStruct((256, 1024), F32),
        ),
        in_specs=[any_spec] * 4,
        out_specs=(any_spec, any_spec),
        scratch_shapes=[
            pltpu.VMEM((64, 128), F32),
            pltpu.VMEM((128, 1024), F32),
            pltpu.VMEM((8, 256, 128), F32),
            pltpu.VMEM((64, 64), F32),
            pltpu.VMEM((2, 8, 32, 128), F32),
            pltpu.VMEM((8, 32, 128), F32),
            pltpu.VMEM((8, 32, 128), F32),
            pltpu.VMEM((8, 2, 32, 32, 128), F32),
            pltpu.VMEM((4, 2, 32, 2048), F32),
            pltpu.VMEM((2, 32, 32, 256), F32),
            pltpu.VMEM((4, 256, 512), BF16),
            pltpu.VMEM((4, 256, 512), BF16),
            pltpu.VMEM((4, 4, 512, 256), BF16),
            pltpu.VMEM((4, 4, 512, 256), BF16),
            dma((4,)),
            dma((8,)),
            dma((8,)),
            dma((8,)),
            dma((8,)),
            dma((4,)),
            dma((4,)),
            dma((4, 8)),
            dma((4, 8)),
            dma((8,)),
            dma((8,)),
            dma((8, 4)),
            dma((8, 4)),
            dma((2, 3, 4)),
            dma((2, 3, 4)),
            dma((1,)),
            dma((1,)),
            dma((8, 4)),
            dma((8, 4)),
        ],
        compiler_params=pltpu.CompilerParams(
            collective_id=0, has_side_effects=True, vmem_limit_bytes=60 * 1024 * 1024
        ),
        name="panel_step",
    )(ft, block_inverse, panel_rhs, trailing_rhs)


def solution(mesh):
    in_specs = (P("reg", "prod"), P("prod", "reg"), P("reg", None), P(("reg", "prod"), None))
    out_specs = (P("prod", "reg"), P(("reg", "prod"), None))
    return jax.shard_map(local, mesh=mesh, in_specs=in_specs, out_specs=out_specs, check_vma=False)
```
